256 devices in a mesh: tgt: 16 (over z, x_hi), src: 16 (over x_lo, y, core).
Axes of the slice: x: 4 (x_hi: 2, x_lo: 2; x = x_hi * 2 + x_lo), y: 4, z: 8, core: 2. Of those that a mesh axis runs over, the one named last changes fastest.
Arguments:
- kernel: bfloat16 [8, 8192, 8192], P(None, 'tgt', 'src'), may hold values from -0.0234375 to 0.0234375
- history: bfloat16 [8, 128, 8192], P(None, None, 'src'), may hold values from -1 to 1
- driving: float32 [128, 8192], P(None, ('tgt', 'src')), may hold values from -6 to 6
- load_rate: float32 [8192], P(('tgt', 'src')), may hold values from -0.3 to 0.3
- rate_gain: float32 [8192], P(('tgt', 'src')), may hold values from 0.3 to 1.2
- friction: float32 [8192], P(('tgt', 'src')), may hold values from 0.2 to 1
- state_decay: float32 [8192], P(('tgt', 'src')), may hold values from 0.3 to 0.95
Outputs:
- stress: float32 [128, 8192], P(None, ('tgt', 'src'))
- state: float32 [128, 8192], P(None, ('tgt', 'src'))
- slip_rate: bfloat16 [128, 8192], P(None, ('tgt', 'src'))
The draws below stay inside these ranges and needn't reach their ends.
All inputs are finite; a program needn't handle non-finite values.
Results may differ from the reference program's by a relative error of at most 0.0032.
Values may be sent and summed in bfloat16 or wider, within the bound.
A program may use at most 64 MiB of HBM per device.

```python
import math
import jax
import jax.numpy as jnp
from jax import lax

E = 8192
LAGS = 8
SCEN = 128
STEPS = 6


def level_of(own_key, extent, cuts, smallest, high):
    def one(position, blocks):
        heights = jax.random.uniform(jax.random.fold_in(jax.random.fold_in(own_key, 6), position), (blocks,), jnp.float32, smallest / len(cuts), high / len(cuts))
        return jnp.repeat(jnp.exp(heights), extent[position] // blocks).reshape((-1,) + (1,) * (len(extent) - position - 1))

    loudness = one(*cuts[0])
    for cut in cuts[1:]:
        loudness = loudness * one(*cut)
    return loudness


def normal_values(own_key, extent, spread, limit, split=(), kind=jnp.bfloat16):
    level = level_of(own_key, extent, split, -0.22, 0.18) if split else 1.0
    array = jax.random.normal(own_key, extent, jnp.float32) * spread * level
    return jnp.minimum(jnp.maximum(array, -limit), limit).astype(kind)


def setup_inputs(seed: int = 0) -> dict:
    seeds = jax.random.split(jax.random.key(seed), 8)
    kernel = normal_values(seeds[0], (LAGS, E, E), (LAGS * E) ** -0.5, 0.0234375, ((1, 16), (2, 16)))
    history = jnp.clip(jax.random.uniform(seeds[1], (LAGS, SCEN, E), jnp.float32, -1.0, 1.0) * level_of(seeds[1], (LAGS, SCEN, E), ((2, 16),), -0.4, 0.0), -1.0, 1.0).astype(jnp.bfloat16)
    driving = normal_values(seeds[2], (SCEN, E), 1.0, 6.0, ((1, 256),), jnp.float32)
    load_rate = jnp.clip(jax.random.uniform(seeds[3], (E,), jnp.float32, -0.3, 0.3) * level_of(seeds[3], (E,), ((0, 256),), -0.4, 0.0), -0.3, 0.3)
    rate_gain = jnp.clip(jnp.exp(math.log(1.2) - 1.3862944 * jax.random.uniform(seeds[4], (E,), jnp.float32) ** level_of(seeds[4], (E,), ((0, 256),), -0.2, 0.2)), 0.3, 1.2)
    friction = jnp.clip(0.2 + 0.8 * jax.random.uniform(seeds[5], (E,), jnp.float32) ** level_of(seeds[5], (E,), ((0, 256),), -0.2, 0.2), 0.2, 1.0)
    state_decay = jnp.clip(0.3 + 0.65 * jax.random.uniform(seeds[6], (E,), jnp.float32) ** level_of(seeds[6], (E,), ((0, 256),), -0.2, 0.2), 0.3, 0.95)
    return {"kernel": kernel, "history": history, "driving": driving, "load_rate": load_rate, "rate_gain": rate_gain, "friction": friction, "state_decay": state_decay}


def reference(kernel, history, driving, load_rate, rate_gain, friction, state_decay):
    state = jnp.zeros(driving.shape, jnp.float32)
    recent = history

    def add_lag(summed, operands):
        lag_kernel, lag_rates = operands
        term = lax.dot_general(lag_rates.astype(jnp.float32), lag_kernel.astype(jnp.float32),
                               (((1,), (1,)), ((), ())), precision=lax.Precision.HIGHEST)
        return summed + term, None

    stress = driving
    slip_rate = history[0]
    for section in range(STEPS):
        summed, _ = lax.scan(add_lag, jnp.zeros(driving.shape, jnp.float32), (kernel, recent))
        stress = driving + (section + 1) * load_rate[None, :] - summed
        slip_rate = jnp.tanh(rate_gain[None, :] * (stress - friction[None, :] * state)).astype(jnp.bfloat16)
        state = state_decay[None, :] * state + slip_rate.astype(jnp.float32)
        recent = jnp.concatenate([slip_rate[None], recent[:-1]], axis=0)
    return stress, state, slip_rate
```

```python
import jax
import jax.numpy as jnp
from jax import lax
from jax.experimental import pallas as pl
from jax.experimental.pallas import tpu as pltpu
from jax.sharding import PartitionSpec as P

MESH = pl.DeviceIdType.MESH
STEPS = 6
LAGS = 8
ROW = 16
CHUNK = 32
SCEN = 128
BLOCK = ROW * CHUNK
ROW_OFFSETS = [
    (dx, dy, dc)
    for dy, dx in ((2, 1), (2, 0), (1, 1), (3, 1), (1, 0), (3, 0), (0, 1), (0, 0))
    for dc in (1, 0)
    if (dx, dy, dc) != (0, 0, 0)
]
Z_OFFSETS = (4, 5, 3, 6, 2, 7, 1, 0)


def march(
    kernel_hbm, history_hbm, driving_ref, load_ref, gain_ref, friction_ref, decay_ref,
    stress_out, state_out, slip_out,
    operator, past, rates, rest, sent, received, fresh,
    load_sem, past_sem, row_send, row_recv, col_send, col_recv,
):
    t, s = lax.axis_index("tgt"), lax.axis_index("src")
    z, x_hi = t // 2, lax.rem(t, 2)
    x_lo, y, core = s // 8, lax.rem(s // 2, 4), lax.rem(s, 2)

    past_copy = pltpu.make_async_copy(history_hbm, past, past_sem)
    past_copy.start()
    loads = [
        pltpu.make_async_copy(kernel_hbm.at[lag], operator.at[lag], load_sem.at[lag])
        for lag in range(LAGS)
    ]
    for copy in loads:
        copy.start()

    barrier = pltpu.get_barrier_semaphore()

    def greet_row(k, carry):
        pl.semaphore_signal(barrier, inc=1, device_id=(t, lax.rem(s + k, ROW)), device_id_type=MESH)
        return carry

    lax.fori_loop(1, ROW, greet_row, 0)

    @pl.when(s != t)
    def _():
        pl.semaphore_signal(barrier, inc=1, device_id=(s, s), device_id_type=MESH)

    def greet_source(k, carry):
        pl.semaphore_signal(barrier, inc=1, device_id=(s, lax.rem(s + k, ROW)), device_id_type=MESH)
        return carry

    lax.fori_loop(1, ROW, greet_source, 0)

    gain = jnp.broadcast_to(gain_ref[...], (SCEN, CHUNK)).T
    friction = jnp.broadcast_to(friction_ref[...], (SCEN, CHUNK)).T
    decay = jnp.broadcast_to(decay_ref[...], (SCEN, CHUNK)).T
    load = jnp.broadcast_to(load_ref[...], (SCEN, CHUNK)).T
    driving = driving_ref[...]

    past_copy.wait()
    for lag in range(LAGS):
        rates[LAGS - 1 - lag] = past[lag].T.reshape(ROW, CHUNK, SCEN)

    def product(lag, slot):
        return jnp.dot(
            operator[lag], rates[slot].reshape(BLOCK, SCEN), preferred_element_type=jnp.float32
        )

    for lag in range(LAGS):
        loads[lag].wait()
        term = product(lag, LAGS - 1 - lag)
        rest[...] = term if lag == 0 else rest[...] + term

    pl.semaphore_wait(barrier, 2 * ROW - 1 - jnp.where(s == t, 1, 0))

    def send_partials(step):
        sent[step] = rest[...].astype(jnp.bfloat16).reshape(ROW, CHUNK, SCEN)
        for k, (dx, dy, dc) in enumerate(ROW_OFFSETS):
            to = lax.rem(x_lo + dx, 2) * 8 + lax.rem(y + dy, 4) * 2 + lax.rem(core + dc, 2)
            pltpu.make_async_remote_copy(
                sent.at[step, to], received.at[step, k], row_send.at[step], row_recv.at[step],
                device_id=(t, to), device_id_type=MESH,
            ).start()

    def update(step, state):
        pltpu.make_async_copy(received.at[step], received.at[step], row_recv.at[step]).wait()
        total = rest[pl.ds(pl.multiple_of(s * CHUNK, CHUNK), CHUNK), :]
        for k in range(ROW - 1):
            total = total + received[step, k].astype(jnp.float32)
        count = lax.convert_element_type(step + 1, jnp.float32)
        stress = driving + count * load - total
        slip = jnp.tanh(gain * (stress - friction * state)).astype(jnp.bfloat16)
        return stress, decay * state + slip.astype(jnp.float32), slip

    def send_rates(step, slip):
        fresh[step] = slip
        slot = step + LAGS
        for dz in Z_OFFSETS:
            for dx in (1, 0):
                to = lax.rem(z + dz, 8) * 2 + lax.rem(x_hi + dx, 2)

                def remote():
                    pltpu.make_async_remote_copy(
                        fresh.at[step], rates.at[slot, s], col_send.at[step], col_recv.at[step],
                        device_id=(to, t), device_id_type=MESH,
                    ).start()

                if dz == 0 and dx == 0:
                    pl.when(s != t)(remote)

                    @pl.when(s == t)
                    def _():
                        pltpu.make_async_copy(
                            fresh.at[step], rates.at[slot, s], col_recv.at[step]
                        ).start()
                else:
                    remote()

    def one_step(step, state):
        send_partials(step)

        def older(lag, carry):
            return carry + product(lag, step + LAGS - lag)

        total = lax.fori_loop(2, LAGS, older, product(1, step + LAGS - 1))
        stress, state, slip = update(step, state)
        send_rates(step, slip)
        slot = step + LAGS
        pltpu.make_async_copy(rates.at[slot], rates.at[slot], col_recv.at[step]).wait()
        rest[...] = total + product(0, slot)
        return state

    state = lax.fori_loop(0, STEPS - 1, one_step, jnp.zeros((CHUNK, SCEN), jnp.float32))
    send_partials(STEPS - 1)
    stress, state, slip = update(STEPS - 1, state)
    stress_out[...] = stress
    state_out[...] = state
    slip_out[...] = slip

    def drain(step, carry):
        pltpu.make_async_copy(received.at[step], received.at[step], row_send.at[step]).wait()
        return carry

    lax.fori_loop(0, STEPS, drain, 0)

    def drain_rates(step, carry):
        part = rates.at[step + LAGS, pl.ds(0, ROW - 1)]
        pltpu.make_async_copy(part, part, col_send.at[step]).wait()

        @pl.when(s != t)
        def _():
            pltpu.make_async_copy(fresh.at[step], fresh.at[step], col_send.at[step]).wait()

        return carry

    lax.fori_loop(0, STEPS - 1, drain_rates, 0)


def shards(kernel, history, driving, load_rate, rate_gain, friction, state_decay):
    vmem = pl.BlockSpec(memory_space=pltpu.VMEM)
    hbm = pl.BlockSpec(memory_space=pltpu.HBM)
    row = lambda v: v.reshape(1, CHUNK)
    outs = pl.pallas_call(
        march,
        name="march",
        out_shape=(
            jax.ShapeDtypeStruct((CHUNK, SCEN), jnp.float32),
            jax.ShapeDtypeStruct((CHUNK, SCEN), jnp.float32),
            jax.ShapeDtypeStruct((CHUNK, SCEN), jnp.bfloat16),
        ),
        in_specs=[hbm, hbm, vmem, vmem, vmem, vmem, vmem],
        out_specs=(vmem, vmem, vmem),
        scratch_shapes=[
            pltpu.VMEM((LAGS, BLOCK, BLOCK), jnp.bfloat16),
            pltpu.VMEM((LAGS, SCEN, BLOCK), jnp.bfloat16),
            pltpu.VMEM((LAGS + STEPS - 1, ROW, CHUNK, SCEN), jnp.bfloat16),
            pltpu.VMEM((BLOCK, SCEN), jnp.float32),
            pltpu.VMEM((STEPS, ROW, CHUNK, SCEN), jnp.bfloat16),
            pltpu.VMEM((STEPS, ROW - 1, CHUNK, SCEN), jnp.bfloat16),
            pltpu.VMEM((STEPS, CHUNK, SCEN), jnp.bfloat16),
            pltpu.SemaphoreType.DMA((LAGS,)),
            pltpu.SemaphoreType.DMA,
            pltpu.SemaphoreType.DMA((STEPS,)),
            pltpu.SemaphoreType.DMA((STEPS,)),
            pltpu.SemaphoreType.DMA((STEPS,)),
            pltpu.SemaphoreType.DMA((STEPS,)),
        ],
        compiler_params=pltpu.CompilerParams(
            collective_id=0, has_side_effects=True, vmem_limit_bytes=60 * 1024 * 1024
        ),
    )(
        kernel, history, driving.T, row(load_rate), row(rate_gain), row(friction), row(state_decay)
    )
    return tuple(out.T for out in outs)


def solution(mesh):
    both = ("tgt", "src")
    return jax.shard_map(
        shards,
        mesh=mesh,
        in_specs=(
            P(None, "tgt", "src"), P(None, None, "src"), P(None, both),
            P(both), P(both), P(both), P(both),
        ),
        out_specs=(P(None, both), P(None, both), P(None, both)),
        check_vma=False,
    )
```

```python
import jax
import jax.numpy as jnp
from jax import lax
from jax.experimental import pallas as pl
from jax.experimental.pallas import tpu as pltpu
from jax.sharding import PartitionSpec as P

MESH = pl.DeviceIdType.MESH
STEPS = 6
LAGS = 8
ROW = 16
CHUNK = 32
SCEN = 128
BLOCK = ROW * CHUNK
ROW_OFFSETS = [
    (dx, dy, dc)
    for dy, dx in ((2, 1), (2, 0), (1, 1), (3, 1), (1, 0), (3, 0), (0, 1), (0, 0))
    for dc in (1, 0)
    if (dx, dy, dc) != (0, 0, 0)
]
Z_OFFSETS = (4, 5, 3, 6, 2, 7, 1, 0)


def march(
    kernel_hbm, history_hbm, driving_hbm, load_hbm, gain_hbm, friction_hbm, decay_hbm,
    total_out, base_out, held_out, gain_out, kept_out,
    operator, past, rates, rest, sent, received, fresh, driving_ref, vectors, results,
    load_sem, past_sem, small_sem, out_sem, row_send, row_recv, col_send, col_recv, open_sem,
):
    t, s = lax.axis_index("tgt"), lax.axis_index("src")
    z, x_hi = t // 2, lax.rem(t, 2)
    x_lo, y, core = s // 8, lax.rem(s // 2, 4), lax.rem(s, 2)

    def mate(offset):
        dx, dy, dc = offset
        return lax.rem(x_lo + dx, 2) * 8 + lax.rem(y + dy, 4) * 2 + lax.rem(core + dc, 2)

    host = lax.rem(t + 8, ROW)
    barrier = pltpu.get_barrier_semaphore()
    pl.semaphore_signal(barrier, inc=1, device_id=(s, lax.rem(s + 8, ROW)), device_id_type=MESH)
    for offset in ROW_OFFSETS:
        pl.semaphore_signal(barrier, inc=1, device_id=(t, mate(offset)), device_id_type=MESH)

    past_copies = [
        pltpu.make_async_copy(history_hbm.at[lag], past.at[lag], past_sem.at[lag])
        for lag in range(LAGS)
    ]
    loads = [
        pltpu.make_async_copy(kernel_hbm.at[lag], operator.at[lag], load_sem.at[lag])
        for lag in range(LAGS)
    ]
    for lag in range(LAGS):
        past_copies[lag].start()
        loads[lag].start()
    smalls = [pltpu.make_async_copy(driving_hbm, driving_ref, small_sem.at[0])]
    for k, vector in enumerate((gain_hbm, friction_hbm, decay_hbm, load_hbm)):
        smalls.append(pltpu.make_async_copy(vector, vectors.at[k], small_sem.at[k + 1]))
    for copy in smalls:
        copy.start()

    def product(lag, slot):
        return jnp.dot(
            operator[lag], rates[slot].reshape(BLOCK, SCEN), preferred_element_type=jnp.float32
        )

    for lag in range(LAGS):
        past_copies[lag].wait()
        rates[LAGS - 1 - lag] = past[lag].T.reshape(ROW, CHUNK, SCEN)
        loads[lag].wait()
        term = product(lag, LAGS - 1 - lag)
        rest[...] = term if lag == 0 else rest[...] + term

    for copy in smalls:
        copy.wait()
    gain, friction, decay, load = [
        jnp.broadcast_to(vectors[k], (SCEN, CHUNK)).T for k in range(4)
    ]
    driving = driving_ref[...]

    pl.semaphore_wait(barrier, ROW - 1 + jnp.where(s == host, ROW, 0))

    def send_partials(step):
        sent[step] = rest[...].astype(jnp.bfloat16).reshape(ROW, CHUNK, SCEN)
        for k, offset in enumerate(ROW_OFFSETS):
            to = mate(offset)
            pltpu.make_async_remote_copy(
                sent.at[step, to], received.at[step, k], row_send.at[step], row_recv.at[step],
                device_id=(t, to), device_id_type=MESH,
            ).start()

    def gathered(step):
        pltpu.make_async_copy(received.at[step], received.at[step], row_recv.at[step]).wait()
        total = rest[pl.ds(pl.multiple_of(s * CHUNK, CHUNK), CHUNK), :]
        for k in range(ROW - 1):
            total = total + received[step, k].astype(jnp.float32)
        return total

    def update(step, state):
        total = gathered(step)
        count = lax.convert_element_type(step + 1, jnp.float32)
        stress = driving + count * load - total
        slip = jnp.tanh(gain * (stress - friction * state)).astype(jnp.bfloat16)
        return decay * state + slip.astype(jnp.float32), slip

    def send_rates(step, slip):
        fresh[step] = slip
        slot = step + LAGS
        for dz in Z_OFFSETS:
            for dx in (1, 0):
                to = lax.rem(z + dz, 8) * 2 + lax.rem(x_hi + dx, 2)

                def remote():
                    pltpu.make_async_remote_copy(
                        fresh.at[step], rates.at[slot, s], col_send.at[step], col_recv.at[step],
                        device_id=(to, t), device_id_type=MESH,
                    ).start()

                if dz == 0 and dx == 0:
                    pl.when(s != t)(remote)

                    @pl.when(s == t)
                    def _():
                        pltpu.make_async_copy(
                            fresh.at[step], rates.at[slot, s], col_recv.at[step]
                        ).start()
                else:
                    remote()

    def one_step(step, state):
        send_partials(step)

        @pl.when((step == 0) & (s == host))
        def _():
            for offset in ROW_OFFSETS:
                pl.semaphore_signal(
                    open_sem, inc=1, device_id=(t, mate(offset)), device_id_type=MESH
                )

        def older(lag, carry):
            return carry + product(lag, step + LAGS - lag)

        total = lax.fori_loop(2, LAGS, older, product(1, step + LAGS - 1))
        state, slip = update(step, state)

        @pl.when((step == 0) & (s != host))
        def _():
            pl.semaphore_wait(open_sem, 1)

        send_rates(step, slip)
        slot = step + LAGS
        pltpu.make_async_copy(rates.at[slot], rates.at[slot], col_recv.at[step]).wait()
        rest[...] = total + product(0, slot)
        return state

    state = lax.fori_loop(0, STEPS - 1, one_step, jnp.zeros((CHUNK, SCEN), jnp.float32))
    send_partials(STEPS - 1)
    results[1] = driving + STEPS * load
    results[2] = friction * state
    results[3] = gain
    results[4] = decay * state
    copies = [
        pltpu.make_async_copy(results.at[k], out, out_sem.at[k])
        for k, out in enumerate((total_out, base_out, held_out, gain_out, kept_out))
    ]
    for copy in copies[1:]:
        copy.start()
    results[0] = gathered(STEPS - 1)
    copies[0].start()

    def drain(step, carry):
        pltpu.make_async_copy(received.at[step], received.at[step], row_send.at[step]).wait()
        return carry

    lax.fori_loop(0, STEPS, drain, 0)

    def drain_rates(step, carry):
        part = rates.at[step + LAGS, pl.ds(0, ROW - 1)]
        pltpu.make_async_copy(part, part, col_send.at[step]).wait()

        @pl.when(s != t)
        def _():
            pltpu.make_async_copy(fresh.at[step], fresh.at[step], col_send.at[step]).wait()

        return carry

    lax.fori_loop(0, STEPS - 1, drain_rates, 0)
    for copy in copies:
        copy.wait()


def shards(kernel, history, driving, load_rate, rate_gain, friction, state_decay):
    hbm = pl.BlockSpec(memory_space=pltpu.HBM)
    row = lambda v: v.reshape(1, CHUNK)
    total, base, held, gain, kept = pl.pallas_call(
        march,
        name="march",
        out_shape=(jax.ShapeDtypeStruct((CHUNK, SCEN), jnp.float32),) * 5,
        in_specs=[hbm] * 7,
        out_specs=(hbm,) * 5,
        scratch_shapes=[
            pltpu.VMEM((LAGS, BLOCK, BLOCK), jnp.bfloat16),
            pltpu.VMEM((LAGS, SCEN, BLOCK), jnp.bfloat16),
            pltpu.VMEM((LAGS + STEPS - 1, ROW, CHUNK, SCEN), jnp.bfloat16),
            pltpu.VMEM((BLOCK, SCEN), jnp.float32),
            pltpu.VMEM((STEPS, ROW, CHUNK, SCEN), jnp.bfloat16),
            pltpu.VMEM((STEPS, ROW - 1, CHUNK, SCEN), jnp.bfloat16),
            pltpu.VMEM((STEPS, CHUNK, SCEN), jnp.bfloat16),
            pltpu.VMEM((CHUNK, SCEN), jnp.float32),
            pltpu.VMEM((4, 1, CHUNK), jnp.float32),
            pltpu.VMEM((5, CHUNK, SCEN), jnp.float32),
            pltpu.SemaphoreType.DMA((LAGS,)),
            pltpu.SemaphoreType.DMA((LAGS,)),
            pltpu.SemaphoreType.DMA((5,)),
            pltpu.SemaphoreType.DMA((5,)),
            pltpu.SemaphoreType.DMA((STEPS,)),
            pltpu.SemaphoreType.DMA((STEPS,)),
            pltpu.SemaphoreType.DMA((STEPS,)),
            pltpu.SemaphoreType.DMA((STEPS,)),
            pltpu.SemaphoreType.REGULAR,
        ],
        compiler_params=pltpu.CompilerParams(
            collective_id=0, has_side_effects=True, vmem_limit_bytes=60 * 1024 * 1024
        ),
    )(
        kernel, history, driving.T, row(load_rate), row(rate_gain), row(friction), row(state_decay)
    )
    stress = base - total
    slip = jnp.tanh(gain * (stress - held)).astype(jnp.bfloat16)
    state = kept + slip.astype(jnp.float32)
    return stress.T, state.T, slip.T


def solution(mesh):
    both = ("tgt", "src")
    return jax.shard_map(
        shards,
        mesh=mesh,
        in_specs=(
            P(None, "tgt", "src"), P(None, None, "src"), P(None, both),
            P(both), P(both), P(both), P(both),
        ),
        out_specs=(P(None, both), P(None, both), P(None, both)),
        check_vma=False,
    )
```

```python
import jax
import jax.numpy as jnp
from jax import lax
from jax.experimental import pallas as pl
from jax.experimental.pallas import tpu as pltpu
from jax.sharding import PartitionSpec as P

MESH = pl.DeviceIdType.MESH
STEPS = 6
LAGS = 8
ROW = 16
CHUNK = 32
SCEN = 128
BLOCK = ROW * CHUNK
ROW_OFFSETS = [
    (dx, dy, dc)
    for dy, dx in ((2, 1), (2, 0), (1, 1), (3, 1), (1, 0), (3, 0), (0, 1), (0, 0))
    for dc in (1, 0)
    if (dx, dy, dc) != (0, 0, 0)
]
Z_OFFSETS = (4, 5, 3, 6, 2, 7, 1, 0)


def march(
    kernel_hbm, history_hbm, driving_hbm, load_hbm, gain_hbm, friction_hbm, decay_hbm,
    total_out, base_out, held_out, gain_out, kept_out,
    operator, past, rates, rest, sent, sent_far, received, fresh, driving_ref, vectors, results,
    load_sem, past_sem, small_sem, out_sem, row_send, row_recv, col_send, col_recv, open_sem,
):
    t, s = lax.axis_index("tgt"), lax.axis_index("src")
    z, x_hi = t // 2, lax.rem(t, 2)
    x_lo, y, core = s // 8, lax.rem(s // 2, 4), lax.rem(s, 2)

    def mate(offset):
        dx, dy, dc = offset
        return lax.rem(x_lo + dx, 2) * 8 + lax.rem(y + dy, 4) * 2 + lax.rem(core + dc, 2)

    host = lax.rem(t + 8, ROW)
    barrier = pltpu.get_barrier_semaphore()
    pl.semaphore_signal(barrier, inc=1, device_id=(s, lax.rem(s + 8, ROW)), device_id_type=MESH)
    for offset in ROW_OFFSETS:
        pl.semaphore_signal(barrier, inc=1, device_id=(t, mate(offset)), device_id_type=MESH)

    past_copies = [
        pltpu.make_async_copy(history_hbm.at[lag], past.at[lag], past_sem.at[lag])
        for lag in range(LAGS)
    ]
    loads = [
        pltpu.make_async_copy(kernel_hbm.at[lag], operator.at[lag], load_sem.at[lag])
        for lag in range(LAGS)
    ]
    for lag in range(LAGS):
        past_copies[lag].start()
        loads[lag].start()
    smalls = [pltpu.make_async_copy(driving_hbm, driving_ref, small_sem.at[0])]
    for k, vector in enumerate((gain_hbm, friction_hbm, decay_hbm, load_hbm)):
        smalls.append(pltpu.make_async_copy(vector, vectors.at[k], small_sem.at[k + 1]))
    for copy in smalls:
        copy.start()

    def product(lag, slot):
        return jnp.dot(
            operator[lag], rates[slot].reshape(BLOCK, SCEN), preferred_element_type=jnp.float32
        )

    for lag in range(LAGS):
        past_copies[lag].wait()
        loads[lag].wait()
        term = lax.dot_general(
            operator[lag], past[lag], (((1,), (1,)), ((), ())), preferred_element_type=jnp.float32
        )
        rest[...] = term if lag == 0 else rest[...] + term

    for copy in smalls:
        copy.wait()
    gain, friction, decay, load = [
        jnp.broadcast_to(vectors[k], (SCEN, CHUNK)).T for k in range(4)
    ]
    driving = driving_ref[...]

    pl.semaphore_wait(barrier, ROW - 1 + jnp.where(s == host, ROW, 0))

    far = lax.rem(x_lo + 1, 2) * 4 + lax.rem(y + 2, 4)
    far_rows = pl.ds(pl.multiple_of(far * 2 * CHUNK, 2 * CHUNK), 2 * CHUNK)
    own_rows = pl.ds(pl.multiple_of(s * CHUNK, CHUNK), CHUNK)

    def send_partial(step, k, source):
        pltpu.make_async_remote_copy(
            source, received.at[step, k], row_send.at[step], row_recv.at[step],
            device_id=(t, mate(ROW_OFFSETS[k])), device_id_type=MESH,
        ).start()

    def send_far(step, partial):
        sent_far[step] = partial.astype(jnp.bfloat16).reshape(2, CHUNK, SCEN)
        for k in range(2):
            send_partial(step, k, sent_far.at[step, lax.rem(core + ROW_OFFSETS[k][2], 2)])

    def send_near(step, partial):
        rest[...] = partial
        sent[step] = partial.astype(jnp.bfloat16).reshape(ROW, CHUNK, SCEN)
        for k in range(2, ROW - 1):
            send_partial(step, k, sent.at[step, mate(ROW_OFFSETS[k])])

    def send_newest(step, slot):
        new = rates[slot].reshape(BLOCK, SCEN)
        send_far(step, rest[far_rows, :] + jnp.dot(
            operator[0, far_rows, :], new, preferred_element_type=jnp.float32
        ))
        send_near(step, rest[...] + jnp.dot(
            operator[0], new, preferred_element_type=jnp.float32
        ))

    def gathered(step):
        pltpu.make_async_copy(received.at[step], received.at[step], row_recv.at[step]).wait()
        parts = [received[step, k].astype(jnp.float32) for k in range(ROW - 1)]
        while len(parts) > 1:
            parts = [sum(parts[k:k + 2][1:], parts[k]) for k in range(0, len(parts), 2)]
        return parts[0]

    def send_rates(step, slip):
        fresh[step] = slip
        slot = step + LAGS
        for dz in Z_OFFSETS:
            for dx in (1, 0):
                to = lax.rem(z + dz, 8) * 2 + lax.rem(x_hi + dx, 2)

                def remote():
                    pltpu.make_async_remote_copy(
                        fresh.at[step], rates.at[slot, s], col_send.at[step], col_recv.at[step],
                        device_id=(to, t), device_id_type=MESH,
                    ).start()

                if dz == 0 and dx == 0:
                    pl.when(s != t)(remote)

                    @pl.when(s == t)
                    def _():
                        pltpu.make_async_copy(
                            fresh.at[step], rates.at[slot, s], col_recv.at[step]
                        ).start()
                else:
                    remote()

    def one_step(step, state):
        @pl.when((step == 0) & (s == host))
        def _():
            for offset in ROW_OFFSETS:
                pl.semaphore_signal(
                    open_sem, inc=1, device_id=(t, mate(offset)), device_id_type=MESH
                )

        count = lax.convert_element_type(step + 1, jnp.float32)
        known = gain * (driving + count * load - friction * state - rest[own_rows, :])
        kept = decay * state

        def older(lag, carry):
            return carry + product(lag, step + LAGS - lag)

        rest[...] = lax.fori_loop(2, LAGS, older, product(1, step + LAGS - 1))

        @pl.when((step == 0) & (s != host))
        def _():
            pl.semaphore_wait(open_sem, 1)

        slip = jnp.tanh(known - gain * gathered(step)).astype(jnp.bfloat16)
        send_rates(step, slip)
        slot = step + LAGS
        pltpu.make_async_copy(rates.at[slot], rates.at[slot], col_recv.at[step]).wait()
        send_newest(step + 1, slot)
        return kept + slip.astype(jnp.float32)

    send_far(0, rest[far_rows, :])
    send_near(0, rest[...])
    for lag in range(LAGS):
        rates[LAGS - 1 - lag] = past[lag].T.reshape(ROW, CHUNK, SCEN)
    state = lax.fori_loop(0, STEPS - 1, one_step, jnp.zeros((CHUNK, SCEN), jnp.float32))
    results[1] = driving + STEPS * load - rest[own_rows, :]
    results[2] = friction * state
    results[3] = gain
    results[4] = decay * state
    copies = [
        pltpu.make_async_copy(results.at[k], out, out_sem.at[k])
        for k, out in enumerate((total_out, base_out, held_out, gain_out, kept_out))
    ]
    for copy in copies[1:]:
        copy.start()
    results[0] = gathered(STEPS - 1)
    copies[0].start()

    def drain(step, carry):
        pltpu.make_async_copy(received.at[step], received.at[step], row_send.at[step]).wait()
        return carry

    lax.fori_loop(0, STEPS, drain, 0)

    def drain_rates(step, carry):
        part = rates.at[step + LAGS, pl.ds(0, ROW - 1)]
        pltpu.make_async_copy(part, part, col_send.at[step]).wait()

        @pl.when(s != t)
        def _():
            pltpu.make_async_copy(fresh.at[step], fresh.at[step], col_send.at[step]).wait()

        return carry

    lax.fori_loop(0, STEPS - 1, drain_rates, 0)
    for copy in copies:
        copy.wait()


def shards(kernel, history, driving, load_rate, rate_gain, friction, state_decay):
    hbm = pl.BlockSpec(memory_space=pltpu.HBM)
    row = lambda v: v.reshape(1, CHUNK)
    total, base, held, gain, kept = pl.pallas_call(
        march,
        name="march",
        out_shape=(jax.ShapeDtypeStruct((CHUNK, SCEN), jnp.float32),) * 5,
        in_specs=[hbm] * 7,
        out_specs=(hbm,) * 5,
        scratch_shapes=[
            pltpu.VMEM((LAGS, BLOCK, BLOCK), jnp.bfloat16),
            pltpu.VMEM((LAGS, SCEN, BLOCK), jnp.bfloat16),
            pltpu.VMEM((LAGS + STEPS - 1, ROW, CHUNK, SCEN), jnp.bfloat16),
            pltpu.VMEM((BLOCK, SCEN), jnp.float32),
            pltpu.VMEM((STEPS, ROW, CHUNK, SCEN), jnp.bfloat16),
            pltpu.VMEM((STEPS, 2, CHUNK, SCEN), jnp.bfloat16),
            pltpu.VMEM((STEPS, ROW - 1, CHUNK, SCEN), jnp.bfloat16),
            pltpu.VMEM((STEPS, CHUNK, SCEN), jnp.bfloat16),
            pltpu.VMEM((CHUNK, SCEN), jnp.float32),
            pltpu.VMEM((4, 1, CHUNK), jnp.float32),
            pltpu.VMEM((5, CHUNK, SCEN), jnp.float32),
            pltpu.SemaphoreType.DMA((LAGS,)),
            pltpu.SemaphoreType.DMA((LAGS,)),
            pltpu.SemaphoreType.DMA((5,)),
            pltpu.SemaphoreType.DMA((5,)),
            pltpu.SemaphoreType.DMA((STEPS,)),
            pltpu.SemaphoreType.DMA((STEPS,)),
            pltpu.SemaphoreType.DMA((STEPS,)),
            pltpu.SemaphoreType.DMA((STEPS,)),
            pltpu.SemaphoreType.REGULAR,
        ],
        compiler_params=pltpu.CompilerParams(
            collective_id=0, has_side_effects=True, vmem_limit_bytes=60 * 1024 * 1024
        ),
    )(
        kernel, history, driving.T, row(load_rate), row(rate_gain), row(friction), row(state_decay)
    )
    stress = base - total
    slip = jnp.tanh(gain * (stress - held)).astype(jnp.bfloat16)
    state = kept + slip.astype(jnp.float32)
    return stress.T, state.T, slip.T


def solution(mesh):
    both = ("tgt", "src")
    return jax.shard_map(
        shards,
        mesh=mesh,
        in_specs=(
            P(None, "tgt", "src"), P(None, None, "src"), P(None, both),
            P(both), P(both), P(both), P(both),
        ),
        out_specs=(P(None, both), P(None, both), P(None, both)),
        check_vma=False,
    )
```

```python
import jax
import jax.numpy as jnp
from jax import lax
from jax.experimental import pallas as pl
from jax.experimental.pallas import tpu as pltpu
from jax.sharding import PartitionSpec as P

MESH = pl.DeviceIdType.MESH
STEPS = 6
LAGS = 8
ROW = 16
CHUNK = 32
SCEN = 128
BLOCK = ROW * CHUNK
ROW_OFFSETS = [
    (dx, dy, dc)
    for dy, dx in ((2, 1), (2, 0), (1, 1), (3, 1), (1, 0), (3, 0), (0, 1), (0, 0))
    for dc in (1, 0)
    if (dx, dy, dc) != (0, 0, 0)
]
Z_OFFSETS = (4, 5, 3, 6, 2, 7, 1, 0)


def march(
    kernel_hbm, history_hbm, driving_hbm, load_hbm, gain_hbm, friction_hbm, decay_hbm,
    total_out, base_out, held_out, gain_out, kept_out,
    operator, past, rates, rest, sent, sent_far, received, fresh, driving_ref, vectors,
    load_sem, past_sem, small_sem, row_send, row_recv, col_send, col_recv, open_sem,
):
    t, s = lax.axis_index("tgt"), lax.axis_index("src")
    z, x_hi = t // 2, lax.rem(t, 2)
    x_lo, y, core = s // 8, lax.rem(s // 2, 4), lax.rem(s, 2)

    def mate(offset):
        dx, dy, dc = offset
        return lax.rem(x_lo + dx, 2) * 8 + lax.rem(y + dy, 4) * 2 + lax.rem(core + dc, 2)

    past_copies = [
        pltpu.make_async_copy(history_hbm.at[lag], past.at[lag], past_sem.at[lag])
        for lag in range(LAGS)
    ]
    loads = [
        pltpu.make_async_copy(kernel_hbm.at[lag], operator.at[lag], load_sem.at[lag])
        for lag in range(LAGS)
    ]
    for lag in range(LAGS):
        past_copies[lag].start()
        loads[lag].start()
    host = lax.rem(t + 8, ROW)
    barrier = pltpu.get_barrier_semaphore()
    pl.semaphore_signal(barrier, inc=1, device_id=(s, lax.rem(s + 8, ROW)), device_id_type=MESH)
    for offset in ROW_OFFSETS:
        pl.semaphore_signal(barrier, inc=1, device_id=(t, mate(offset)), device_id_type=MESH)

    smalls = [pltpu.make_async_copy(driving_hbm, driving_ref, small_sem.at[0])]
    for k, vector in enumerate((gain_hbm, friction_hbm, decay_hbm, load_hbm)):
        smalls.append(pltpu.make_async_copy(vector, vectors.at[k], small_sem.at[k + 1]))
    for copy in smalls:
        copy.start()

    def product(lag, slot):
        return jnp.dot(
            operator[lag], rates[slot].reshape(BLOCK, SCEN), preferred_element_type=jnp.float32
        )

    for lag in range(LAGS):
        past_copies[lag].wait()
        loads[lag].wait()
        term = lax.dot_general(
            operator[lag], past[lag], (((1,), (1,)), ((), ())), preferred_element_type=jnp.float32
        )
        rest[...] = term if lag == 0 else rest[...] + term

    for copy in smalls:
        copy.wait()
    gain, friction, decay, load = [
        jnp.broadcast_to(vectors[k], (SCEN, CHUNK)).T for k in range(4)
    ]
    driving = driving_ref[...]

    pl.semaphore_wait(barrier, ROW - 1 + jnp.where(s == host, ROW, 0))

    far = lax.rem(x_lo + 1, 2) * 4 + lax.rem(y + 2, 4)
    far_rows = pl.ds(pl.multiple_of(far * 2 * CHUNK, 2 * CHUNK), 2 * CHUNK)
    own_rows = pl.ds(pl.multiple_of(s * CHUNK, CHUNK), CHUNK)

    def send_partial(step, k, source):
        pltpu.make_async_remote_copy(
            source, received.at[step, k], row_send.at[step], row_recv.at[step],
            device_id=(t, mate(ROW_OFFSETS[k])), device_id_type=MESH,
        ).start()

    def send_far(step, partial):
        sent_far[step] = partial.astype(jnp.bfloat16).reshape(2, CHUNK, SCEN)
        for k in range(2):
            send_partial(step, k, sent_far.at[step, lax.rem(core + ROW_OFFSETS[k][2], 2)])

    def send_near(step, partial):
        rest[...] = partial
        sent[step] = partial.astype(jnp.bfloat16).reshape(ROW, CHUNK, SCEN)
        for k in range(2, ROW - 1):
            send_partial(step, k, sent.at[step, mate(ROW_OFFSETS[k])])

    def send_newest(step, slot):
        new = rates[slot].reshape(BLOCK, SCEN)
        send_far(step, rest[far_rows, :] + jnp.dot(
            operator[0, far_rows, :], new, preferred_element_type=jnp.float32
        ))
        send_near(step, rest[...] + jnp.dot(
            operator[0], new, preferred_element_type=jnp.float32
        ))

    def gathered(step):
        pltpu.make_async_copy(received.at[step], received.at[step], row_recv.at[step]).wait()
        parts = [received[step, k].astype(jnp.float32) for k in range(ROW - 1)]
        while len(parts) > 1:
            parts = [sum(parts[k:k + 2][1:], parts[k]) for k in range(0, len(parts), 2)]
        return parts[0]

    def send_rates(step, slip):
        fresh[step] = slip
        slot = step + LAGS
        for dz in Z_OFFSETS:
            for dx in (1, 0):
                to = lax.rem(z + dz, 8) * 2 + lax.rem(x_hi + dx, 2)

                def remote():
                    pltpu.make_async_remote_copy(
                        fresh.at[step], rates.at[slot, s], col_send.at[step], col_recv.at[step],
                        device_id=(to, t), device_id_type=MESH,
                    ).start()

                if dz == 0 and dx == 0:
                    pl.when(s != t)(remote)

                    @pl.when(s == t)
                    def _():
                        pltpu.make_async_copy(
                            fresh.at[step], rates.at[slot, s], col_recv.at[step]
                        ).start()
                else:
                    remote()

    def one_step(step, state):
        @pl.when((step == 0) & (s == host))
        def _():
            for offset in ROW_OFFSETS:
                pl.semaphore_signal(
                    open_sem, inc=1, device_id=(t, mate(offset)), device_id_type=MESH
                )

        count = lax.convert_element_type(step + 1, jnp.float32)
        known = gain * (driving + count * load - friction * state - rest[own_rows, :])
        kept = decay * state

        def older(lag, carry):
            return carry + product(lag, step + LAGS - lag)

        rest[...] = lax.fori_loop(2, LAGS, older, product(1, step + LAGS - 1))

        @pl.when((step == 0) & (s != host))
        def _():
            pl.semaphore_wait(open_sem, 1)

        slip = jnp.tanh(known - gain * gathered(step)).astype(jnp.bfloat16)
        send_rates(step, slip)
        slot = step + LAGS
        pltpu.make_async_copy(rates.at[slot], rates.at[slot], col_recv.at[step]).wait()
        send_newest(step + 1, slot)
        return kept + slip.astype(jnp.float32)

    send_far(0, rest[far_rows, :])
    send_near(0, rest[...])
    for lag in range(LAGS):
        rates[LAGS - 1 - lag] = past[lag].T.reshape(ROW, CHUNK, SCEN)
    state = lax.fori_loop(0, STEPS - 1, one_step, jnp.zeros((CHUNK, SCEN), jnp.float32))
    base_out[...] = driving + STEPS * load - rest[own_rows, :]
    held_out[...] = friction * state
    gain_out[...] = gain
    kept_out[...] = decay * state
    total_out[...] = gathered(STEPS - 1)

    def drain(step, carry):
        pltpu.make_async_copy(received.at[step], received.at[step], row_send.at[step]).wait()
        return carry

    lax.fori_loop(0, STEPS, drain, 0)

    def drain_rates(step, carry):
        part = rates.at[step + LAGS, pl.ds(0, ROW - 1)]
        pltpu.make_async_copy(part, part, col_send.at[step]).wait()

        @pl.when(s != t)
        def _():
            pltpu.make_async_copy(fresh.at[step], fresh.at[step], col_send.at[step]).wait()

        return carry

    lax.fori_loop(0, STEPS - 1, drain_rates, 0)


def shards(kernel, history, driving, load_rate, rate_gain, friction, state_decay):
    hbm = pl.BlockSpec(memory_space=pltpu.HBM)
    row = lambda v: v.reshape(1, CHUNK)
    total, base, held, gain, kept = pl.pallas_call(
        march,
        name="march",
        out_shape=(pltpu.VMEM((CHUNK, SCEN), jnp.float32),) * 5,
        in_specs=[hbm] * 7,
        out_specs=(pl.BlockSpec(memory_space=pltpu.VMEM),) * 5,
        scratch_shapes=[
            pltpu.VMEM((LAGS, BLOCK, BLOCK), jnp.bfloat16),
            pltpu.VMEM((LAGS, SCEN, BLOCK), jnp.bfloat16),
            pltpu.VMEM((LAGS + STEPS - 1, ROW, CHUNK, SCEN), jnp.bfloat16),
            pltpu.VMEM((BLOCK, SCEN), jnp.float32),
            pltpu.VMEM((STEPS, ROW, CHUNK, SCEN), jnp.bfloat16),
            pltpu.VMEM((STEPS, 2, CHUNK, SCEN), jnp.bfloat16),
            pltpu.VMEM((STEPS, ROW - 1, CHUNK, SCEN), jnp.bfloat16),
            pltpu.VMEM((STEPS, CHUNK, SCEN), jnp.bfloat16),
            pltpu.VMEM((CHUNK, SCEN), jnp.float32),
            pltpu.VMEM((4, 1, CHUNK), jnp.float32),
            pltpu.SemaphoreType.DMA((LAGS,)),
            pltpu.SemaphoreType.DMA((LAGS,)),
            pltpu.SemaphoreType.DMA((5,)),
            pltpu.SemaphoreType.DMA((STEPS,)),
            pltpu.SemaphoreType.DMA((STEPS,)),
            pltpu.SemaphoreType.DMA((STEPS,)),
            pltpu.SemaphoreType.DMA((STEPS,)),
            pltpu.SemaphoreType.REGULAR,
        ],
        compiler_params=pltpu.CompilerParams(
            collective_id=0, has_side_effects=True, vmem_limit_bytes=60 * 1024 * 1024
        ),
    )(*(
        pltpu.with_memory_space_constraint(array, pltpu.HBM)
        for array in (
            kernel, history, driving.T,
            row(load_rate), row(rate_gain), row(friction), row(state_decay),
        )
    ))
    stress = base - total
    slip = jnp.tanh(gain * (stress - held)).astype(jnp.bfloat16)
    state = kept + slip.astype(jnp.float32)
    return stress.T, state.T, slip.T


def solution(mesh):
    both = ("tgt", "src")
    return jax.shard_map(
        shards,
        mesh=mesh,
        in_specs=(
            P(None, "tgt", "src"), P(None, None, "src"), P(None, both),
            P(both), P(both), P(both), P(both),
        ),
        out_specs=(P(None, both), P(None, both), P(None, both)),
        check_vma=False,
    )
```

```python
import jax
import jax.numpy as jnp
from jax import lax
from jax.experimental import pallas as pl
from jax.experimental.pallas import tpu as pltpu
from jax.sharding import PartitionSpec as P

MESH = pl.DeviceIdType.MESH
STEPS = 6
LAGS = 8
ROW = 16
CHUNK = 32
SCEN = 128
BLOCK = ROW * CHUNK
BANDS = [slice(start, start + 128) for start in range(0, BLOCK, 128)]
ROW_OFFSETS = [
    (dx, dy, dc)
    for dy, dx in ((2, 1), (2, 0), (1, 1), (3, 1), (1, 0), (3, 0), (0, 1), (0, 0))
    for dc in (1, 0)
    if (dx, dy, dc) != (0, 0, 0)
]
Z_OFFSETS = (4, 5, 3, 6, 2, 7, 1, 0)


def march(
    kernel_hbm, history_hbm, driving_hbm, load_hbm, gain_hbm, friction_hbm, decay_hbm,
    total_out, base_out, held_out, gain_out, kept_out,
    operator, past, rates, rest, sent, sent_far, received, fresh, driving_ref, vectors,
    load_sem, past_sem, small_sem, row_send, row_recv, col_send, col_recv, open_sem,
):
    t, s = lax.axis_index("tgt"), lax.axis_index("src")
    z, x_hi = t // 2, lax.rem(t, 2)
    x_lo, y, core = s // 8, lax.rem(s // 2, 4), lax.rem(s, 2)

    def mate(offset):
        dx, dy, dc = offset
        return lax.rem(x_lo + dx, 2) * 8 + lax.rem(y + dy, 4) * 2 + lax.rem(core + dc, 2)

    past_copies = [
        pltpu.make_async_copy(history_hbm.at[lag], past.at[lag], past_sem.at[lag])
        for lag in range(LAGS)
    ]
    loads = [
        pltpu.make_async_copy(kernel_hbm.at[lag], operator.at[lag], load_sem.at[lag])
        for lag in range(LAGS)
    ]
    for lag in range(LAGS):
        past_copies[lag].start()
        loads[lag].start()
    mates = [mate(offset) for offset in ROW_OFFSETS]
    host = lax.rem(t + 8, ROW)
    barrier = pltpu.get_barrier_semaphore()
    pl.semaphore_signal(barrier, inc=1, device_id=(s, lax.rem(s + 8, ROW)), device_id_type=MESH)
    for to in mates:
        pl.semaphore_signal(barrier, inc=1, device_id=(t, to), device_id_type=MESH)

    smalls = [pltpu.make_async_copy(driving_hbm, driving_ref, small_sem.at[0])]
    for k, vector in enumerate((gain_hbm, friction_hbm, decay_hbm, load_hbm)):
        smalls.append(pltpu.make_async_copy(vector, vectors.at[k], small_sem.at[k + 1]))
    for copy in smalls:
        copy.start()

    def product(lag, slot):
        return jnp.dot(
            operator[lag], rates[slot].reshape(BLOCK, SCEN), preferred_element_type=jnp.float32
        )

    for lag in range(LAGS):
        past_copies[lag].wait()
        loads[lag].wait()
        for rows in BANDS:
            term = lax.dot_general(
                operator[lag, rows, :], past[lag], (((1,), (1,)), ((), ())),
                preferred_element_type=jnp.float32,
            )
            rest[rows, :] = term if lag == 0 else rest[rows, :] + term

    pl.semaphore_wait(barrier, ROW - 1 + jnp.where(s == host, ROW, 0))

    far = lax.rem(x_lo + 1, 2) * 4 + lax.rem(y + 2, 4)
    far_rows = pl.ds(pl.multiple_of(far * 2 * CHUNK, 2 * CHUNK), 2 * CHUNK)
    own_rows = pl.ds(pl.multiple_of(s * CHUNK, CHUNK), CHUNK)

    def send_partial(step, k, source):
        pltpu.make_async_remote_copy(
            source, received.at[step, k], row_send.at[step], row_recv.at[step],
            device_id=(t, mates[k]), device_id_type=MESH,
        ).start()

    def send_far(step, partial):
        sent_far[step] = partial.astype(jnp.bfloat16).reshape(2, CHUNK, SCEN)
        for k in range(2):
            send_partial(step, k, sent_far.at[step, lax.rem(core + ROW_OFFSETS[k][2], 2)])

    def send_near(step, new=None):
        for band, rows in enumerate(BANDS):
            partial = rest[rows, :]
            if new is not None:
                partial = partial + jnp.dot(
                    operator[0, rows, :], new, preferred_element_type=jnp.float32
                )
                rest[rows, :] = partial
            sent[step, 4 * band:4 * band + 4] = partial.astype(jnp.bfloat16).reshape(4, CHUNK, SCEN)
        for k in range(2, ROW - 1):
            send_partial(step, k, sent.at[step, mates[k]])

    def send_newest(step, slot):
        new = rates[slot].reshape(BLOCK, SCEN)
        send_far(step, rest[far_rows, :] + jnp.dot(
            operator[0, far_rows, :], new, preferred_element_type=jnp.float32
        ))
        send_near(step, new)

    def gathered(step):
        pltpu.make_async_copy(received.at[step], received.at[step], row_recv.at[step]).wait()
        parts = [received[step, k].astype(jnp.float32) for k in range(ROW - 1)]
        while len(parts) > 1:
            parts = [sum(parts[k:k + 2][1:], parts[k]) for k in range(0, len(parts), 2)]
        return parts[0]

    column = {
        (dz, dx): lax.rem(z + dz, 8) * 2 + lax.rem(x_hi + dx, 2)
        for dz in Z_OFFSETS for dx in (1, 0)
    }

    def send_rates(step, slip):
        fresh[step] = slip
        slot = step + LAGS
        for dz in Z_OFFSETS:
            for dx in (1, 0):
                to = column[dz, dx]

                def remote():
                    pltpu.make_async_remote_copy(
                        fresh.at[step], rates.at[slot, s], col_send.at[step], col_recv.at[step],
                        device_id=(to, t), device_id_type=MESH,
                    ).start()

                if dz == 0 and dx == 0:
                    pl.when(s != t)(remote)

                    @pl.when(s == t)
                    def _():
                        pltpu.make_async_copy(
                            fresh.at[step], rates.at[slot, s], col_recv.at[step]
                        ).start()
                else:
                    remote()

    def one_step(step, state):
        @pl.when((step == 0) & (s == host))
        def _():
            for offset in ROW_OFFSETS:
                pl.semaphore_signal(
                    open_sem, inc=1, device_id=(t, mate(offset)), device_id_type=MESH
                )

        count = lax.convert_element_type(step + 1, jnp.float32)
        known = gain * (driving + count * load - friction * state - rest[own_rows, :])
        kept = decay * state

        def older(lag, carry):
            return carry + product(lag, step + LAGS - lag)

        rest[...] = lax.fori_loop(2, LAGS, older, product(1, step + LAGS - 1))

        @pl.when((step == 0) & (s != host))
        def _():
            pl.semaphore_wait(open_sem, 1)

        slip = jnp.tanh(known - gain * gathered(step)).astype(jnp.bfloat16)
        send_rates(step, slip)
        slot = step + LAGS
        pltpu.make_async_copy(rates.at[slot], rates.at[slot], col_recv.at[step]).wait()
        send_newest(step + 1, slot)
        return kept + slip.astype(jnp.float32)

    send_far(0, rest[far_rows, :])
    send_near(0)
    for copy in smalls:
        copy.wait()
    gain, friction, decay, load = [
        jnp.broadcast_to(vectors[k], (SCEN, CHUNK)).T for k in range(4)
    ]
    driving = driving_ref[...]

    for lag in range(LAGS):
        rates[LAGS - 1 - lag] = past[lag].T.reshape(ROW, CHUNK, SCEN)
    state = lax.fori_loop(0, STEPS - 1, one_step, jnp.zeros((CHUNK, SCEN), jnp.float32))
    base_out[...] = driving + STEPS * load - rest[own_rows, :]
    held_out[...] = friction * state
    gain_out[...] = gain
    kept_out[...] = decay * state
    def drain(step, carry):
        pltpu.make_async_copy(received.at[step], received.at[step], row_send.at[step]).wait()
        return carry

    lax.fori_loop(0, STEPS - 1, drain, 0)

    def drain_rates(step, carry):
        part = rates.at[step + LAGS, pl.ds(0, ROW - 1)]
        pltpu.make_async_copy(part, part, col_send.at[step]).wait()

        @pl.when(s != t)
        def _():
            pltpu.make_async_copy(fresh.at[step], fresh.at[step], col_send.at[step]).wait()

        return carry

    lax.fori_loop(0, STEPS - 1, drain_rates, 0)

    total_out[...] = gathered(STEPS - 1)
    drain(STEPS - 1, 0)


def shards(kernel, history, driving, load_rate, rate_gain, friction, state_decay):
    hbm = pl.BlockSpec(memory_space=pltpu.HBM)
    row = lambda v: v.reshape(1, CHUNK)
    total, base, held, gain, kept = pl.pallas_call(
        march,
        name="march",
        out_shape=(pltpu.VMEM((CHUNK, SCEN), jnp.float32),) * 5,
        in_specs=[hbm] * 7,
        out_specs=(pl.BlockSpec(memory_space=pltpu.VMEM),) * 5,
        scratch_shapes=[
            pltpu.VMEM((LAGS, BLOCK, BLOCK), jnp.bfloat16),
            pltpu.VMEM((LAGS, SCEN, BLOCK), jnp.bfloat16),
            pltpu.VMEM((LAGS + STEPS - 1, ROW, CHUNK, SCEN), jnp.bfloat16),
            pltpu.VMEM((BLOCK, SCEN), jnp.float32),
            pltpu.VMEM((STEPS, ROW, CHUNK, SCEN), jnp.bfloat16),
            pltpu.VMEM((STEPS, 2, CHUNK, SCEN), jnp.bfloat16),
            pltpu.VMEM((STEPS, ROW - 1, CHUNK, SCEN), jnp.bfloat16),
            pltpu.VMEM((STEPS, CHUNK, SCEN), jnp.bfloat16),
            pltpu.VMEM((CHUNK, SCEN), jnp.float32),
            pltpu.VMEM((4, 1, CHUNK), jnp.float32),
            pltpu.SemaphoreType.DMA((LAGS,)),
            pltpu.SemaphoreType.DMA((LAGS,)),
            pltpu.SemaphoreType.DMA((5,)),
            pltpu.SemaphoreType.DMA((STEPS,)),
            pltpu.SemaphoreType.DMA((STEPS,)),
            pltpu.SemaphoreType.DMA((STEPS,)),
            pltpu.SemaphoreType.DMA((STEPS,)),
            pltpu.SemaphoreType.REGULAR,
        ],
        compiler_params=pltpu.CompilerParams(
            collective_id=0, has_side_effects=True, vmem_limit_bytes=60 * 1024 * 1024
        ),
    )(*(
        pltpu.with_memory_space_constraint(array, pltpu.HBM)
        for array in (
            kernel, history, driving.T,
            row(load_rate), row(rate_gain), row(friction), row(state_decay),
        )
    ))
    stress = base - total
    slip = jnp.tanh(gain * (stress - held)).astype(jnp.bfloat16)
    state = kept + slip.astype(jnp.float32)
    return stress.T, state.T, slip.T


def solution(mesh):
    both = ("tgt", "src")
    return jax.shard_map(
        shards,
        mesh=mesh,
        in_specs=(
            P(None, "tgt", "src"), P(None, None, "src"), P(None, both),
            P(both), P(both), P(both), P(both),
        ),
        out_specs=(P(None, both), P(None, both), P(None, both)),
        check_vma=False,
    )
```

```python
import jax
import jax.numpy as jnp
from jax import lax
from jax.experimental import pallas as pl
from jax.experimental.pallas import tpu as pltpu
from jax.sharding import PartitionSpec as P

MESH = pl.DeviceIdType.MESH
STEPS = 6
LAGS = 8
ROW = 16
CHUNK = 32
SCEN = 128
BLOCK = ROW * CHUNK
BANDS = [slice(start, start + 128) for start in range(0, BLOCK, 128)]
ROW_OFFSETS = [
    (dx, dy, dc)
    for dy, dx in ((2, 1), (2, 0), (1, 1), (3, 1), (1, 0), (3, 0), (0, 1), (0, 0))
    for dc in (1, 0)
    if (dx, dy, dc) != (0, 0, 0)
]
SLIP_OFFSETS = [
    (dz, dx) for pair in ((4,), (3, 5), (2, 6), (1, 7), (0,)) for dx in (1, 0) for dz in pair
]


def march(
    kernel_hbm, history_hbm, driving_hbm, load_hbm, gain_hbm, friction_hbm, decay_hbm,
    total_out, base_out, held_out, gain_out, kept_out,
    operator, past, rates, rest, sent, sent_far, received, fresh, driving_ref, vectors,
    load_sem, past_sem, small_sem, row_send, row_recv, col_send, col_recv, open_sem,
):
    t, s = lax.axis_index("tgt"), lax.axis_index("src")
    z, x_hi = t // 2, lax.rem(t, 2)
    x_lo, y, core = s // 8, lax.rem(s // 2, 4), lax.rem(s, 2)

    def mate(offset):
        dx, dy, dc = offset
        return lax.rem(x_lo + dx, 2) * 8 + lax.rem(y + dy, 4) * 2 + lax.rem(core + dc, 2)

    past_copies = [
        pltpu.make_async_copy(history_hbm.at[lag], past.at[lag], past_sem.at[lag])
        for lag in range(LAGS)
    ]
    loads = [
        pltpu.make_async_copy(kernel_hbm.at[lag], operator.at[lag], load_sem.at[lag])
        for lag in range(LAGS)
    ]
    for lag in range(LAGS):
        past_copies[lag].start()
        loads[lag].start()
    mates = [mate(offset) for offset in ROW_OFFSETS]
    host = lax.rem(t + 8, ROW)
    barrier = pltpu.get_barrier_semaphore()
    pl.semaphore_signal(barrier, inc=1, device_id=(s, lax.rem(s + 8, ROW)), device_id_type=MESH)
    for to in mates:
        pl.semaphore_signal(barrier, inc=1, device_id=(t, to), device_id_type=MESH)

    smalls = [pltpu.make_async_copy(driving_hbm, driving_ref, small_sem.at[0])]
    for k, vector in enumerate((gain_hbm, friction_hbm, decay_hbm, load_hbm)):
        smalls.append(pltpu.make_async_copy(vector, vectors.at[k], small_sem.at[k + 1]))
    for copy in smalls:
        copy.start()

    def product(lag, slot):
        return jnp.dot(
            operator[lag], rates[slot].reshape(BLOCK, SCEN), preferred_element_type=jnp.float32
        )

    rest[...] = jnp.zeros_like(rest)

    def first(lag, carry):
        pltpu.make_async_copy(history_hbm.at[lag], past.at[lag], past_sem.at[lag]).wait()
        pltpu.make_async_copy(kernel_hbm.at[lag], operator.at[lag], load_sem.at[lag]).wait()
        for rows in BANDS:
            rest[rows, :] += lax.dot_general(
                operator[lag, rows, :], past[lag], (((1,), (1,)), ((), ())),
                preferred_element_type=jnp.float32,
            )
        return carry

    lax.fori_loop(0, LAGS, first, 0)
    pl.semaphore_wait(barrier, ROW - 1 + jnp.where(s == host, ROW, 0))

    far = lax.rem(x_lo + 1, 2) * 4 + lax.rem(y + 2, 4)
    far_rows = pl.ds(pl.multiple_of(far * 2 * CHUNK, 2 * CHUNK), 2 * CHUNK)
    own_rows = pl.ds(pl.multiple_of(s * CHUNK, CHUNK), CHUNK)

    def send_partial(step, k, source):
        pltpu.make_async_remote_copy(
            source, received.at[step, k], row_send.at[step], row_recv.at[step],
            device_id=(t, mates[k]), device_id_type=MESH,
        ).start()

    def send_far(step, partial):
        sent_far[step] = partial.astype(jnp.bfloat16).reshape(2, CHUNK, SCEN)
        for k in range(2):
            send_partial(step, k, sent_far.at[step, lax.rem(core + ROW_OFFSETS[k][2], 2)])

    def send_near(step, new=None):
        for band, rows in enumerate(BANDS):
            partial = rest[rows, :]
            if new is not None:
                partial = partial + jnp.dot(
                    operator[0, rows, :], new, preferred_element_type=jnp.float32
                )
                rest[rows, :] = partial
            sent[step, 4 * band:4 * band + 4] = partial.astype(jnp.bfloat16).reshape(4, CHUNK, SCEN)
        for k in range(2, ROW - 1):
            send_partial(step, k, sent.at[step, mates[k]])

    def send_newest(step, slot):
        new = rates[slot].reshape(BLOCK, SCEN)
        send_far(step, rest[far_rows, :] + jnp.dot(
            operator[0, far_rows, :], new, preferred_element_type=jnp.float32
        ))
        send_near(step, new)

    def gathered(step):
        pltpu.make_async_copy(received.at[step], received.at[step], row_recv.at[step]).wait()
        parts = [received[step, k].astype(jnp.float32) for k in range(ROW - 1)]
        while len(parts) > 1:
            parts = [sum(parts[k:k + 2][1:], parts[k]) for k in range(0, len(parts), 2)]
        return parts[0]

    column = {
        (dz, dx): lax.rem(z + dz, 8) * 2 + lax.rem(x_hi + dx, 2) for dz, dx in SLIP_OFFSETS
    }

    def send_rates(step, slip):
        fresh[step] = slip
        slot = step + LAGS
        for dz, dx in SLIP_OFFSETS:
            to = column[dz, dx]

            def remote():
                pltpu.make_async_remote_copy(
                    fresh.at[step], rates.at[slot, s], col_send.at[step], col_recv.at[step],
                    device_id=(to, t), device_id_type=MESH,
                ).start()

            if dz == 0 and dx == 0:
                pl.when(s != t)(remote)

                @pl.when(s == t)
                def _():
                    pltpu.make_async_copy(
                        fresh.at[step], rates.at[slot, s], col_recv.at[step]
                    ).start()
            else:
                remote()

    def one_step(step, state):
        @pl.when((step == 0) & (s == host))
        def _():
            for offset in ROW_OFFSETS:
                pl.semaphore_signal(
                    open_sem, inc=1, device_id=(t, mate(offset)), device_id_type=MESH
                )

        count = lax.convert_element_type(step + 1, jnp.float32)
        known = gain * (driving + count * load - friction * state - rest[own_rows, :])
        kept = decay * state

        def older(lag, carry):
            return carry + product(lag, step + LAGS - lag)

        rest[...] = lax.fori_loop(2, LAGS, older, product(1, step + LAGS - 1))

        @pl.when((step == 0) & (s != host))
        def _():
            pl.semaphore_wait(open_sem, 1)

        slip = jnp.tanh(known - gain * gathered(step)).astype(jnp.bfloat16)
        send_rates(step, slip)
        slot = step + LAGS
        pltpu.make_async_copy(rates.at[slot], rates.at[slot], col_recv.at[step]).wait()
        send_newest(step + 1, slot)
        return kept + slip.astype(jnp.float32)

    send_far(0, rest[far_rows, :])
    send_near(0)
    for copy in smalls:
        copy.wait()
    gain, friction, decay, load = [
        jnp.broadcast_to(vectors[k], (SCEN, CHUNK)).T for k in range(4)
    ]
    driving = driving_ref[...]


    def turn(lag, carry):
        rates[LAGS - 1 - lag] = past[lag].T.reshape(ROW, CHUNK, SCEN)
        return carry

    lax.fori_loop(0, LAGS, turn, 0)
    state = lax.fori_loop(0, STEPS - 1, one_step, jnp.zeros((CHUNK, SCEN), jnp.float32))
    base_out[...] = driving + STEPS * load - rest[own_rows, :]
    held_out[...] = friction * state
    gain_out[...] = gain
    kept_out[...] = decay * state
    def drain(step, carry):
        pltpu.make_async_copy(received.at[step], received.at[step], row_send.at[step]).wait()
        return carry

    lax.fori_loop(0, STEPS - 1, drain, 0)

    def drain_rates(step, carry):
        part = rates.at[step + LAGS, pl.ds(0, ROW - 1)]
        pltpu.make_async_copy(part, part, col_send.at[step]).wait()

        @pl.when(s != t)
        def _():
            pltpu.make_async_copy(fresh.at[step], fresh.at[step], col_send.at[step]).wait()

        return carry

    lax.fori_loop(0, STEPS - 1, drain_rates, 0)

    total_out[...] = gathered(STEPS - 1)
    drain(STEPS - 1, 0)


def shards(kernel, history, driving, load_rate, rate_gain, friction, state_decay):
    hbm = pl.BlockSpec(memory_space=pltpu.HBM)
    row = lambda v: v.reshape(1, CHUNK)
    total, base, held, gain, kept = pl.pallas_call(
        march,
        name="march",
        out_shape=(pltpu.VMEM((CHUNK, SCEN), jnp.float32),) * 5,
        in_specs=[hbm] * 7,
        out_specs=(pl.BlockSpec(memory_space=pltpu.VMEM),) * 5,
        scratch_shapes=[
            pltpu.VMEM((LAGS, BLOCK, BLOCK), jnp.bfloat16),
            pltpu.VMEM((LAGS, SCEN, BLOCK), jnp.bfloat16),
            pltpu.VMEM((LAGS + STEPS - 1, ROW, CHUNK, SCEN), jnp.bfloat16),
            pltpu.VMEM((BLOCK, SCEN), jnp.float32),
            pltpu.VMEM((STEPS, ROW, CHUNK, SCEN), jnp.bfloat16),
            pltpu.VMEM((STEPS, 2, CHUNK, SCEN), jnp.bfloat16),
            pltpu.VMEM((STEPS, ROW - 1, CHUNK, SCEN), jnp.bfloat16),
            pltpu.VMEM((STEPS, CHUNK, SCEN), jnp.bfloat16),
            pltpu.VMEM((CHUNK, SCEN), jnp.float32),
            pltpu.VMEM((4, 1, CHUNK), jnp.float32),
            pltpu.SemaphoreType.DMA((LAGS,)),
            pltpu.SemaphoreType.DMA((LAGS,)),
            pltpu.SemaphoreType.DMA((5,)),
            pltpu.SemaphoreType.DMA((STEPS,)),
            pltpu.SemaphoreType.DMA((STEPS,)),
            pltpu.SemaphoreType.DMA((STEPS,)),
            pltpu.SemaphoreType.DMA((STEPS,)),
            pltpu.SemaphoreType.REGULAR,
        ],
        compiler_params=pltpu.CompilerParams(
            collective_id=0, has_side_effects=True, vmem_limit_bytes=60 * 1024 * 1024
        ),
    )(*(
        pltpu.with_memory_space_constraint(array, pltpu.HBM)
        for array in (
            kernel, history, driving.T,
            row(load_rate), row(rate_gain), row(friction), row(state_decay),
        )
    ))
    stress = base - total
    slip = jnp.tanh(gain * (stress - held)).astype(jnp.bfloat16)
    state = kept + slip.astype(jnp.float32)
    return stress.T, state.T, slip.T


def solution(mesh):
    both = ("tgt", "src")
    return jax.shard_map(
        shards,
        mesh=mesh,
        in_specs=(
            P(None, "tgt", "src"), P(None, None, "src"), P(None, both),
            P(both), P(both), P(both), P(both),
        ),
        out_specs=(P(None, both), P(None, both), P(None, both)),
        check_vma=False,
    )
```

```python
import jax
import jax.numpy as jnp
from jax import lax
from jax.experimental import pallas as pl
from jax.experimental.pallas import tpu as pltpu
from jax.sharding import PartitionSpec as P

MESH = pl.DeviceIdType.MESH
STEPS = 6
LAGS = 8
ROW = 16
CHUNK = 32
SCEN = 128
BLOCK = ROW * CHUNK
BANDS = [slice(start, start + 128) for start in range(0, BLOCK, 128)]
ROW_OFFSETS = [
    (dx, dy, dc)
    for dy, dx in ((2, 1), (2, 0), (1, 1), (3, 1), (1, 0), (3, 0), (0, 1), (0, 0))
    for dc in (1, 0)
    if (dx, dy, dc) != (0, 0, 0)
]
SLIP_OFFSETS = [
    (dz, dx) for pair in ((4,), (3, 5), (2, 6), (1, 7), (0,)) for dx in (1, 0) for dz in pair
]


def march(
    kernel_hbm, history_hbm, driving_hbm, load_hbm, gain_hbm, friction_hbm, decay_hbm,
    total_out, base_out, held_out, gain_out, kept_out,
    operator, past, rates, rest, sent, sent_far, received, fresh, driving_ref, vectors,
    load_sem, past_sem, small_sem, row_send, row_recv, col_send, col_recv, open_sem,
):
    t, s = lax.axis_index("tgt"), lax.axis_index("src")
    z, x_hi = t // 2, lax.rem(t, 2)
    x_lo, y, core = s // 8, lax.rem(s // 2, 4), lax.rem(s, 2)

    def mate(offset):
        dx, dy, dc = offset
        return lax.rem(x_lo + dx, 2) * 8 + lax.rem(y + dy, 4) * 2 + lax.rem(core + dc, 2)

    past_copies = [
        pltpu.make_async_copy(history_hbm.at[lag], past.at[lag], past_sem.at[lag])
        for lag in range(LAGS)
    ]
    loads = [
        pltpu.make_async_copy(kernel_hbm.at[lag], operator.at[lag], load_sem.at[lag])
        for lag in range(LAGS)
    ]
    for lag in range(LAGS):
        past_copies[lag].start()
        loads[lag].start()
    mates = [mate(offset) for offset in ROW_OFFSETS]
    host = lax.rem(t + 8, ROW)
    barrier = pltpu.get_barrier_semaphore()
    pl.semaphore_signal(barrier, inc=1, device_id=(s, lax.rem(s + 8, ROW)), device_id_type=MESH)
    for to in mates:
        pl.semaphore_signal(barrier, inc=1, device_id=(t, to), device_id_type=MESH)

    smalls = [pltpu.make_async_copy(driving_hbm, driving_ref, small_sem.at[0])]
    for k, vector in enumerate((gain_hbm, friction_hbm, decay_hbm, load_hbm)):
        smalls.append(pltpu.make_async_copy(vector, vectors.at[k], small_sem.at[k + 1]))
    for copy in smalls:
        copy.start()

    rest[...] = jnp.zeros_like(rest)

    def first(lag, carry):
        pltpu.make_async_copy(history_hbm.at[lag], past.at[lag], past_sem.at[lag]).wait()
        pltpu.make_async_copy(kernel_hbm.at[lag], operator.at[lag], load_sem.at[lag]).wait()
        for rows in BANDS:
            rest[rows, :] += lax.dot_general(
                operator[lag, rows, :], past[lag], (((1,), (1,)), ((), ())),
                preferred_element_type=jnp.float32,
            )
        return carry

    lax.fori_loop(0, LAGS, first, 0)
    pl.semaphore_wait(barrier, ROW - 1 + jnp.where(s == host, ROW, 0))

    far = lax.rem(x_lo + 1, 2) * 4 + lax.rem(y + 2, 4)
    far_rows = pl.ds(pl.multiple_of(far * 2 * CHUNK, 2 * CHUNK), 2 * CHUNK)
    own_rows = pl.ds(pl.multiple_of(s * CHUNK, CHUNK), CHUNK)

    def send_partial(step, k, source):
        pltpu.make_async_remote_copy(
            source, received.at[step, k], row_send.at[step], row_recv.at[step],
            device_id=(t, mates[k]), device_id_type=MESH,
        ).start()

    def send_far(step, partial):
        sent_far[step] = partial.astype(jnp.bfloat16).reshape(2, CHUNK, SCEN)
        for k in range(2):
            send_partial(step, k, sent_far.at[step, lax.rem(core + ROW_OFFSETS[k][2], 2)])

    def send_near(step, new=None):
        for band, rows in enumerate(BANDS):
            partial = rest[rows, :]
            if new is not None:
                partial = partial + jnp.dot(
                    operator[0, rows, :], new, preferred_element_type=jnp.float32
                )
                rest[rows, :] = partial
            sent[step, 4 * band:4 * band + 4] = partial.astype(jnp.bfloat16).reshape(4, CHUNK, SCEN)
        for k in range(2, ROW - 1):
            send_partial(step, k, sent.at[step, mates[k]])

    def send_newest(step, slot):
        new = rates[slot].reshape(BLOCK, SCEN)
        send_far(step, rest[far_rows, :] + jnp.dot(
            operator[0, far_rows, :], new, preferred_element_type=jnp.float32
        ))
        send_near(step, new)

    def gathered(step):
        pltpu.make_async_copy(received.at[step], received.at[step], row_recv.at[step]).wait()
        parts = [received[step, k].astype(jnp.float32) for k in range(ROW - 1)]
        while len(parts) > 1:
            parts = [sum(parts[k:k + 2][1:], parts[k]) for k in range(0, len(parts), 2)]
        return parts[0]

    column = {
        (dz, dx): lax.rem(z + dz, 8) * 2 + lax.rem(x_hi + dx, 2) for dz, dx in SLIP_OFFSETS
    }

    def send_rates(step, slip):
        fresh[step] = slip
        slot = step + LAGS
        for dz, dx in SLIP_OFFSETS:
            to = column[dz, dx]

            def remote():
                pltpu.make_async_remote_copy(
                    fresh.at[step], rates.at[slot, s], col_send.at[step], col_recv.at[step],
                    device_id=(to, t), device_id_type=MESH,
                ).start()

            if dz == 0 and dx == 0:
                pl.when(s != t)(remote)

                @pl.when(s == t)
                def _():
                    pltpu.make_async_copy(
                        fresh.at[step], rates.at[slot, s], col_recv.at[step]
                    ).start()
            else:
                remote()

    def one_step(step, state):
        @pl.when((step == 0) & (s == host))
        def _():
            for offset in ROW_OFFSETS:
                pl.semaphore_signal(
                    open_sem, inc=1, device_id=(t, mate(offset)), device_id_type=MESH
                )

        count = lax.convert_element_type(step + 1, jnp.float32)
        known = gain * (driving + count * load - friction * state - rest[own_rows, :])
        kept = decay * state

        def older(band, carry):
            rows = pl.ds(pl.multiple_of(band * 128, 128), 128)
            rest[rows, :] = sum(
                jnp.dot(
                    operator[lag, rows, :], rates[step + LAGS - lag].reshape(BLOCK, SCEN),
                    preferred_element_type=jnp.float32,
                )
                for lag in range(1, LAGS)
            )
            return carry

        lax.fori_loop(0, len(BANDS), older, 0)

        @pl.when((step == 0) & (s != host))
        def _():
            pl.semaphore_wait(open_sem, 1)

        slip = jnp.tanh(known - gain * gathered(step)).astype(jnp.bfloat16)
        send_rates(step, slip)
        slot = step + LAGS
        pltpu.make_async_copy(rates.at[slot], rates.at[slot], col_recv.at[step]).wait()
        send_newest(step + 1, slot)
        return kept + slip.astype(jnp.float32)

    send_far(0, rest[far_rows, :])
    send_near(0)
    for copy in smalls:
        copy.wait()
    gain, friction, decay, load = [
        jnp.broadcast_to(vectors[k], (SCEN, CHUNK)).T for k in range(4)
    ]
    driving = driving_ref[...]


    def turn(lag, carry):
        rates[LAGS - 1 - lag] = past[lag].T.reshape(ROW, CHUNK, SCEN)
        return carry

    lax.fori_loop(0, LAGS, turn, 0)
    state = lax.fori_loop(0, STEPS - 1, one_step, jnp.zeros((CHUNK, SCEN), jnp.float32))
    base_out[...] = driving + STEPS * load - rest[own_rows, :]
    held_out[...] = friction * state
    gain_out[...] = gain
    kept_out[...] = decay * state
    def drain(step, carry):
        pltpu.make_async_copy(received.at[step], received.at[step], row_send.at[step]).wait()
        return carry

    lax.fori_loop(0, STEPS - 1, drain, 0)

    def drain_rates(step, carry):
        part = rates.at[step + LAGS, pl.ds(0, ROW - 1)]
        pltpu.make_async_copy(part, part, col_send.at[step]).wait()

        @pl.when(s != t)
        def _():
            pltpu.make_async_copy(fresh.at[step], fresh.at[step], col_send.at[step]).wait()

        return carry

    lax.fori_loop(0, STEPS - 1, drain_rates, 0)

    total_out[...] = gathered(STEPS - 1)
    drain(STEPS - 1, 0)


def shards(kernel, history, driving, load_rate, rate_gain, friction, state_decay):
    hbm = pl.BlockSpec(memory_space=pltpu.HBM)
    row = lambda v: v.reshape(1, CHUNK)
    total, base, held, gain, kept = pl.pallas_call(
        march,
        name="march",
        out_shape=(pltpu.VMEM((CHUNK, SCEN), jnp.float32),) * 5,
        in_specs=[hbm] * 7,
        out_specs=(pl.BlockSpec(memory_space=pltpu.VMEM),) * 5,
        scratch_shapes=[
            pltpu.VMEM((LAGS, BLOCK, BLOCK), jnp.bfloat16),
            pltpu.VMEM((LAGS, SCEN, BLOCK), jnp.bfloat16),
            pltpu.VMEM((LAGS + STEPS - 1, ROW, CHUNK, SCEN), jnp.bfloat16),
            pltpu.VMEM((BLOCK, SCEN), jnp.float32),
            pltpu.VMEM((STEPS, ROW, CHUNK, SCEN), jnp.bfloat16),
            pltpu.VMEM((STEPS, 2, CHUNK, SCEN), jnp.bfloat16),
            pltpu.VMEM((STEPS, ROW - 1, CHUNK, SCEN), jnp.bfloat16),
            pltpu.VMEM((STEPS, CHUNK, SCEN), jnp.bfloat16),
            pltpu.VMEM((CHUNK, SCEN), jnp.float32),
            pltpu.VMEM((4, 1, CHUNK), jnp.float32),
            pltpu.SemaphoreType.DMA((LAGS,)),
            pltpu.SemaphoreType.DMA((LAGS,)),
            pltpu.SemaphoreType.DMA((5,)),
            pltpu.SemaphoreType.DMA((STEPS,)),
            pltpu.SemaphoreType.DMA((STEPS,)),
            pltpu.SemaphoreType.DMA((STEPS,)),
            pltpu.SemaphoreType.DMA((STEPS,)),
            pltpu.SemaphoreType.REGULAR,
        ],
        compiler_params=pltpu.CompilerParams(
            collective_id=0, has_side_effects=True, vmem_limit_bytes=60 * 1024 * 1024
        ),
    )(*(
        pltpu.with_memory_space_constraint(array, pltpu.HBM)
        for array in (
            kernel, history, driving.T,
            row(load_rate), row(rate_gain), row(friction), row(state_decay),
        )
    ))
    stress = base - total
    slip = jnp.tanh(gain * (stress - held)).astype(jnp.bfloat16)
    state = kept + slip.astype(jnp.float32)
    return stress.T, state.T, slip.T


def solution(mesh):
    both = ("tgt", "src")
    return jax.shard_map(
        shards,
        mesh=mesh,
        in_specs=(
            P(None, "tgt", "src"), P(None, None, "src"), P(None, both),
            P(both), P(both), P(both), P(both),
        ),
        out_specs=(P(None, both), P(None, both), P(None, both)),
        check_vma=False,
    )
```
